512 devices in a mesh: ctx: 64 (over z, x, core), head: 8 (over y).
Axes of the slice: x: 4, y: 8, z: 8, core: 2. Of those that a mesh axis runs over, the one named last changes fastest.
Arguments:
- latents: bfloat16 [512, 2048], P('ctx'), may hold values from -40 to 40
- context: bfloat16 [16384, 2048], P('ctx', 'head'), may hold values from -40 to 40
- lengths: int32 [512], replicated, may hold values from 1 to 16384, as said below
- w_query: bfloat16 [2048, 2048], P(None, 'head'), may hold values from -1 to 1
- w_key: bfloat16 [2048, 2048], P(None, 'head'), may hold values from -1 to 1
- w_value: bfloat16 [2048, 2048], P(None, 'head'), may hold values from -0.125 to 0.125
- w_out: bfloat16 [2048, 2048], P('head'), may hold values from -0.25 to 0.25
Outputs:
- mixed: bfloat16 [512, 2048], P('ctx', 'head')
The draws below stay inside these ranges and needn't reach their ends.
Inputs may be any that keep to these rules, and one draw needn't show every extreme that they name: `lengths`: some latent sees all 16384 positions and some latent only the first.
All inputs are finite; a program needn't handle non-finite values.
Results may differ from the reference program's by a relative error of at most 0.0095.
The reference program's roundings to bfloat16 on the way count: a program that leaves them out, or rounds other values in their place, can miss the bound.
Values may be sent and summed in bfloat16 or wider, within the bound.
No kernel may reach another device: no remote copies, remote signals or barrier semaphores. Data moves between devices by JAX's collectives and lax.ppermute only.
A program may use at most 128 MiB of HBM per device.

```python
import jax
import jax.numpy as jnp
from jax import lax

D = 2048
H = 16
HD = 128
CTX_DEV = 256
L = 512
CONTEXT = 16384
N_CTX = 64


def query_matrix(base):
    return jax.random.normal(jax.random.fold_in(base, 91), (D, H * HD), jnp.float32) * (1.6 * D ** (-0.5))


def draw_latents(key, part):
    key = jax.random.fold_in(key, 1)
    rows = jax.random.normal(key, (L, D), jnp.float32)
    return jnp.clip(rows, -40.0, 40.0).astype(jnp.bfloat16)


def draw_context(key, part):
    key = jax.random.fold_in(key, 2)
    rows = jax.random.normal(key, (CONTEXT, D), jnp.float32)
    return jnp.clip(rows, -40.0, 40.0).astype(jnp.bfloat16)


def draw_w_query(key, part):
    base = key
    key = jax.random.fold_in(key, 3)
    order = jax.random.permutation(key, H)
    ladder = 16.0 ** (order.astype(jnp.float32) / (H - 1))
    matrix = query_matrix(base).reshape(D, H, HD) * ladder[None, :, None]
    return jnp.clip(matrix.reshape(D, H * HD), -1.0, 1.0).astype(jnp.bfloat16)


def draw_w_key(key, part):
    key = jax.random.fold_in(key, 4)
    fresh = jax.random.normal(key, (D, H * HD), jnp.float32) * (1.6 * D ** (-0.5))
    return jnp.clip(fresh, -1.0, 1.0).astype(jnp.bfloat16)


def draw_lengths(key, part):
    key = jax.random.fold_in(key, 6)
    lens = jax.random.randint(key, (L,), 1, CONTEXT + 1)
    first = jax.random.randint(jax.random.fold_in(key, 7), (), 0, L)
    other = (first + 1 + jax.random.randint(jax.random.fold_in(key, 8), (), 0, L - 1)) % L
    places = jnp.arange(L, dtype=jnp.int32)
    lens = jnp.where(places == first, CONTEXT, lens)
    lens = jnp.where(places == other, 1, lens)
    return lens.astype(jnp.int32)


def block_scale(own_key, dims, shards, smallest, top_value):
    loudness, own = 1.0, jax.random.fold_in(own_key, 6)
    for dim, shards_of in shards:
        steps = jnp.exp(jax.random.uniform(jax.random.fold_in(own, dim), (shards_of,), jnp.float32, smallest / len(shards), top_value / len(shards)))
        loudness = loudness * jnp.repeat(steps, dims[dim] // shards_of).reshape([-1 if axis == dim else 1 for axis in range(len(dims))])
    return loudness


def centred(key, dims, spread, bound, pieces=(), held_as=jnp.bfloat16):
    gain = block_scale(key, dims, pieces, -0.22, 0.18) if pieces else 1.0
    result = jax.random.normal(key, dims, jnp.float32) * spread * gain
    return jnp.minimum(jnp.maximum(result, -bound), bound).astype(held_as)


def setup_inputs(seed: int = 0) -> dict:
    seeds = jax.random.split(jax.random.key(seed), 8)
    return {
        "latents": draw_latents(jax.random.fold_in(seeds[7], 71), 0),
        "context": draw_context(jax.random.fold_in(seeds[7], 71), 0),
        "lengths": draw_lengths(jax.random.fold_in(seeds[7], 71), 0),
        "w_query": draw_w_query(jax.random.fold_in(seeds[7], 71), 0),
        "w_key": draw_w_key(jax.random.fold_in(seeds[7], 71), 0),
        "w_value": centred(seeds[5], (D, H * HD), D ** -0.5, 0.125, ((1, 8),)),
        "w_out": centred(seeds[6], (H * HD, D), (H * HD // 4) ** -0.5, 0.25, ((0, 8),)),
    }


def slab_attention(queries, lens, keys, values, positions):
    scores = jnp.einsum('bhd,chd->hbc', queries.astype(jnp.float32), keys.astype(jnp.float32))
    visible = positions[None, :] < lens[:, None]
    scores = jnp.where(visible[None], scores, -jnp.inf)
    top = jnp.maximum(jnp.max(scores, axis=2), -1e30)
    probs = jnp.exp(scores - top[:, :, None]).astype(jnp.bfloat16)
    total = jnp.sum(probs.astype(jnp.float32), axis=2)
    out = jnp.einsum('hbc,chd->bhd', probs.astype(jnp.float32), values.astype(jnp.float32))
    return top, total, out


def combine(first, second):
    top_a, total_a, out_a = first
    top_b, total_b, out_b = second
    top = jnp.maximum(top_a, top_b)
    scale_a = jnp.exp(top_a - top)
    scale_b = jnp.exp(top_b - top)
    total = scale_a * total_a + scale_b * total_b
    out = out_a * scale_a.T[:, :, None] + out_b * scale_b.T[:, :, None]
    return top, total, out


def reference(latents, context, lengths, w_query, w_key, w_value, w_out):
    qscale = 1.0 / (HD ** 0.5)
    queries = (jnp.dot(latents, w_query, preferred_element_type=jnp.float32) * qscale).astype(jnp.bfloat16)
    queries = queries.reshape(L, H, HD)
    slabs = context.reshape(N_CTX, CTX_DEV, D)

    def step(carry, item):
        slab, index = item
        keys = jnp.dot(slab, w_key, preferred_element_type=jnp.float32).astype(jnp.bfloat16).reshape(CTX_DEV, H, HD)
        values = jnp.dot(slab, w_value, preferred_element_type=jnp.float32).astype(jnp.bfloat16).reshape(CTX_DEV, H, HD)
        positions = index * CTX_DEV + jnp.arange(CTX_DEV, dtype=jnp.int32)
        part = slab_attention(queries, lengths, keys, values, positions)
        return combine(carry, part), None

    init = (jnp.full((H, L), -1e30, jnp.float32), jnp.zeros((H, L), jnp.float32), jnp.zeros((L, H, HD), jnp.float32))
    (top, total, out), unused = lax.scan(step, init, (slabs, jnp.arange(N_CTX, dtype=jnp.int32)))
    attended = (out / total.T[:, :, None]).reshape(L, H * HD).astype(jnp.bfloat16)
    projected = jnp.dot(attended, w_out, preferred_element_type=jnp.float32)
    return (latents.astype(jnp.float32) + projected).astype(jnp.bfloat16)
```

```python
import jax
import jax.numpy as jnp
from jax import lax
from jax.sharding import PartitionSpec as P

HD = 128
PAD = 128
BF = jnp.bfloat16
F32 = jnp.float32


def split3(a):
    hi = lax.reduce_precision(a, 8, 7)
    rest = a - hi
    mid = lax.reduce_precision(rest, 8, 7)
    return hi.astype(BF), mid.astype(BF), (rest - mid).astype(BF)


def join3(hi, mid, lo):
    return hi.astype(F32) + (mid.astype(F32) + lo.astype(F32))


def on_device(latents, context, lengths, w_query, w_key, w_value, w_out):
    lat_dev = latents.shape[0]
    groups = lax.axis_size("ctx")
    heads_axis = lax.axis_size("head")
    latent_count = lat_dev * groups
    width = w_query.shape[1]
    heads = width // HD
    ctx_dev = context.shape[0]
    qscale = 1.0 / HD**0.5

    piece = lax.all_gather(context, "head", axis=1, tiled=True)

    local_q = (jnp.dot(latents, w_query, preferred_element_type=F32) * qscale).astype(BF)
    queries = lax.all_to_all(
        jnp.broadcast_to(local_q[None], (groups, lat_dev, width)), "ctx", 0, 0
    )
    queries = queries.reshape(latent_count, heads, HD)

    keys = jnp.dot(piece, w_key, preferred_element_type=F32).astype(BF).reshape(ctx_dev, heads, HD)
    values = jnp.dot(piece, w_value, preferred_element_type=F32).astype(BF).reshape(ctx_dev, heads, HD)
    positions = lax.axis_index("ctx") * ctx_dev + jnp.arange(ctx_dev, dtype=jnp.int32)
    scores = jnp.einsum("bhd,chd->hbc", queries, keys, preferred_element_type=F32)
    visible = positions[None, :] < lengths[:, None]
    scores = jnp.where(visible[None], scores, -jnp.inf)
    top = jnp.maximum(jnp.max(scores, axis=2), -1e30)
    probs = jnp.exp(scores - top[:, :, None]).astype(BF)
    total = jnp.sum(probs.astype(F32), axis=2)
    out = jnp.einsum("hbc,chd->bhd", probs, values, preferred_element_type=F32)

    cols = [p[h][:, None] for h in range(heads) for p in split3(top) + split3(total)]
    meta = jnp.concatenate(cols, axis=1)
    meta = jnp.pad(meta, ((0, 0), (0, PAD - meta.shape[1])))
    packed = jnp.concatenate([out.reshape(latent_count, width).astype(BF), meta], axis=1)
    got = lax.all_to_all(packed.reshape(groups, lat_dev, width + PAD), "ctx", 0, 0)

    parts = []
    for h in range(heads):
        m = got[:, :, width + 6 * h : width + 6 * h + 6]
        t = join3(m[..., 0:1], m[..., 1:2], m[..., 2:3])
        n = join3(m[..., 3:4], m[..., 4:5], m[..., 5:6])
        scale = jnp.exp(t - jnp.max(t, axis=0, keepdims=True))
        o = jnp.sum(scale * got[:, :, h * HD : (h + 1) * HD].astype(F32), axis=0)
        parts.append((o / jnp.sum(scale * n, axis=0)).astype(BF))
    attended = jnp.concatenate(parts, axis=1)

    projected = jnp.dot(attended, w_out, preferred_element_type=F32)
    cols_dev = projected.shape[1] // heads_axis
    shares = projected.reshape(lat_dev, heads_axis, cols_dev).transpose(1, 0, 2)
    summed = jnp.sum(lax.all_to_all(shares, "head", 0, 0), axis=0)
    first_col = lax.axis_index("head") * cols_dev
    residual = lax.dynamic_slice_in_dim(latents, first_col, cols_dev, 1).astype(F32)
    return (residual + summed).astype(BF)


def solution(mesh):
    in_specs = (
        P("ctx", None),
        P("ctx", "head"),
        P(),
        P(None, "head"),
        P(None, "head"),
        P(None, "head"),
        P("head", None),
    )
    return jax.shard_map(
        on_device, mesh=mesh, in_specs=in_specs, out_specs=P("ctx", "head"), check_vma=False
    )
```

```python
import jax
import jax.numpy as jnp
from jax import lax
from jax.experimental import pallas as pl
from jax.experimental.pallas import tpu as pltpu
from jax.sharding import PartitionSpec as P

HD = 128
META = 128
CORES = 2
BF = jnp.bfloat16
F32 = jnp.float32
LIMIT = 40 * 1024 * 1024


def split3(a):
    hi = a.astype(BF).astype(F32)
    rest = a - hi
    mid = rest.astype(BF).astype(F32)
    return [hi, mid, (rest - mid).astype(BF).astype(F32)]


def pack_meta(tops, totals):
    rows = tops[0].shape[0]
    lane = lax.broadcasted_iota(jnp.int32, (rows, META), 1)
    meta = jnp.zeros((rows, META), F32)
    column = 0
    for top, total in zip(tops, totals):
        for part in split3(top) + split3(total):
            meta = jnp.where(lane == column, part, meta)
            column += 1
    return meta.astype(BF)


def read_meta(meta, head):
    m = meta.astype(F32)
    part = [m[..., 6 * head + i : 6 * head + i + 1] for i in range(6)]
    return part[0] + (part[1] + part[2]), part[3] + (part[4] + part[5])


def attend_kernel(place, x, wk, wv, q, lens, keep, send):
    core, base = place[0], place[1]
    heads = wk.shape[1] // HD
    rows, width = q.shape[1], q.shape[2]
    positions = x.shape[1]
    feats = jnp.concatenate([x[f] for f in range(x.shape[0])], axis=1)
    k = jnp.dot(feats, wk[...], preferred_element_type=F32).astype(BF)
    v = jnp.dot(feats, wv[...], preferred_element_type=F32).astype(BF)
    ones = jnp.ones((positions, HD), BF)
    pos = base + lax.broadcasted_iota(jnp.int32, (rows, positions), 1)
    for half, ref in ((1 - core, send), (core, keep)):
        visible = pos < lens[half]
        qh = q[half]
        tops, totals = [], []
        for h in range(heads):
            cols = slice(h * HD, (h + 1) * HD)
            s = lax.dot_general(
                qh[:, cols], k[:, cols], (((1,), (1,)), ((), ())), preferred_element_type=F32
            )
            s = jnp.where(visible, s, -jnp.inf)
            top = jnp.maximum(jnp.max(s, axis=1, keepdims=True), -1e30)
            probs = jnp.exp(s - top).astype(BF)
            both = jnp.dot(
                probs, jnp.concatenate([v[:, cols], ones], axis=1), preferred_element_type=F32
            )
            ref[:, cols] = both[:, :HD].astype(ref.dtype)
            tops.append(top)
            totals.append(both[:, HD : HD + 1])
        ref[:, width:] = pack_meta(tops, totals).astype(ref.dtype)


def pair_kernel(place, keep, got, out):
    other = 1 - place[0]
    width = keep.shape[1] - META
    theirs = got[other]
    tops, totals = [], []
    for h in range(width // HD):
        cols = slice(h * HD, (h + 1) * HD)
        top_a, total_a = read_meta(keep[:, width:], h)
        top_b, total_b = read_meta(theirs[:, width:], h)
        top = jnp.maximum(top_a, top_b)
        scale_a, scale_b = jnp.exp(top_a - top), jnp.exp(top_b - top)
        out[:, cols] = (scale_a * keep[:, cols] + scale_b * theirs[:, cols].astype(F32)).astype(BF)
        tops.append(top)
        totals.append(scale_a * total_a + scale_b * total_b)
    out[:, width:] = pack_meta(tops, totals)


def project_kernel(got, w_out, out):
    width = w_out.shape[0]
    parts = []
    for h in range(width // HD):
        top, total = read_meta(got[:, :, width:], h)
        scale = jnp.exp(top - jnp.max(top, axis=0, keepdims=True))
        o = jnp.sum(scale * got[:, :, h * HD : (h + 1) * HD].astype(F32), axis=0)
        parts.append((o / jnp.sum(scale * total, axis=0)).astype(BF))
    projected = jnp.dot(jnp.concatenate(parts, axis=1), w_out[...], preferred_element_type=F32)
    cols = out.shape[2]
    for d in range(out.shape[0]):
        out[d] = projected[:, d * cols : (d + 1) * cols]


def call(kernel, shapes, n_in, smem_first):
    vmem = pl.BlockSpec(memory_space=pltpu.VMEM)
    specs = [vmem] * n_in
    if smem_first:
        specs[0] = pl.BlockSpec(memory_space=pltpu.SMEM)
    return pl.pallas_call(
        kernel,
        out_shape=shapes,
        in_specs=specs,
        out_specs=jax.tree.map(lambda _: vmem, shapes),
        compiler_params=pltpu.CompilerParams(vmem_limit_bytes=LIMIT),
    )


def on_device(latents, context, lengths, w_query, w_key, w_value, w_out):
    lat_dev = latents.shape[0]
    groups = lax.axis_size("ctx")
    heads_axis = lax.axis_size("head")
    width = w_query.shape[1]
    ctx_dev = context.shape[0]
    chips = groups // CORES
    half = chips * lat_dev
    qscale = 1.0 / HD**0.5
    me = lax.axis_index("ctx")
    place = jnp.stack([me % CORES, me * ctx_dev]).astype(jnp.int32)
    same_core = [[c + CORES * g for g in range(chips)] for c in range(CORES)]
    core_pairs = [[CORES * g + c for c in range(CORES)] for g in range(chips)]

    x = lax.all_to_all(
        jnp.broadcast_to(context[None], (heads_axis,) + context.shape), "head", 0, 0
    )

    q = (jnp.dot(latents, w_query, preferred_element_type=F32) * qscale).astype(BF)
    bit = CORES
    while bit < groups:
        pairs = [[i, i | bit] for i in range(groups) if not i & bit]
        q = lax.all_gather(q, "ctx", axis=0, tiled=True, axis_index_groups=pairs)
        bit *= 2
    q = lax.all_gather(q, "ctx", axis=0, axis_index_groups=core_pairs)
    lens = lengths.reshape(chips, CORES, lat_dev).transpose(1, 0, 2).reshape(CORES, half, 1)

    keep, send = call(
        attend_kernel,
        [
            jax.ShapeDtypeStruct((half, width + META), F32),
            jax.ShapeDtypeStruct((half, width + META), BF),
        ],
        6,
        True,
    )(place, x, w_key, w_value, q, lens)
    got = lax.all_gather(send, "ctx", axis=0, axis_index_groups=core_pairs)
    paired = call(pair_kernel, jax.ShapeDtypeStruct((half, width + META), BF), 3, True)(
        place, keep, got
    )
    got = lax.all_to_all(
        paired.reshape(chips, lat_dev, width + META), "ctx", 0, 0, axis_index_groups=same_core
    )
    cols_dev = w_out.shape[1] // heads_axis
    shares = call(
        project_kernel, jax.ShapeDtypeStruct((heads_axis, lat_dev, cols_dev), F32), 2, False
    )(got, w_out)
    summed = jnp.sum(lax.all_to_all(shares, "head", 0, 0), axis=0)
    first_col = lax.axis_index("head") * cols_dev
    residual = lax.dynamic_slice_in_dim(latents, first_col, cols_dev, 1).astype(F32)
    return (residual + summed).astype(BF)


def solution(mesh):
    in_specs = (
        P("ctx", None),
        P("ctx", "head"),
        P(),
        P(None, "head"),
        P(None, "head"),
        P(None, "head"),
        P("head", None),
    )
    return jax.shard_map(
        on_device, mesh=mesh, in_specs=in_specs, out_specs=P("ctx", "head"), check_vma=False
    )
```

```python
import jax
import jax.numpy as jnp
from jax import lax
from jax.experimental import pallas as pl
from jax.experimental.pallas import tpu as pltpu
from jax.sharding import PartitionSpec as P

HD = 128
META = 128
CORES = 2
LAST = 4
BF = jnp.bfloat16
F32 = jnp.float32
LIMIT = 40 * 1024 * 1024


def split3(a):
    hi = a.astype(BF).astype(F32)
    rest = a - hi
    mid = rest.astype(BF).astype(F32)
    return [hi, mid, (rest - mid).astype(BF).astype(F32)]


def pack_meta(tops, totals):
    rows = tops[0].shape[0]
    lane = lax.broadcasted_iota(jnp.int32, (rows, META), 1)
    meta = jnp.zeros((rows, META), F32)
    column = 0
    for top, total in zip(tops, totals):
        for part in split3(top) + split3(total):
            meta = jnp.where(lane == column, part, meta)
            column += 1
    return meta.astype(BF)


def read_meta(meta, head):
    m = meta.astype(F32)
    part = [m[..., 6 * head + i : 6 * head + i + 1] for i in range(6)]
    return part[0] + (part[1] + part[2]), part[3] + (part[4] + part[5])


def copies_kernel(context, out):
    for d in range(out.shape[0]):
        out[d] = context[...]


def key_value_kernel(x, wk, wv, out):
    width = wk.shape[1]
    feats = jnp.concatenate([x[f] for f in range(x.shape[0])], axis=1)
    out[:, :width] = jnp.dot(feats, wk[...], preferred_element_type=F32).astype(BF)
    out[:, width:] = jnp.dot(feats, wv[...], preferred_element_type=F32).astype(BF)


def attend_kernel(place, kv, q, lens, out):
    core, base = place[0], place[1]
    rows, width = q.shape
    positions = kv.shape[0]
    ones = jnp.ones((positions, HD), BF)
    pos = base + lax.broadcasted_iota(jnp.int32, (rows, positions), 1)
    visible = pos < lens[core]
    tops, totals = [], []
    for h in range(width // HD):
        cols = slice(h * HD, (h + 1) * HD)
        s = lax.dot_general(
            q[:, cols], kv[:, cols], (((1,), (1,)), ((), ())), preferred_element_type=F32
        )
        s = jnp.where(visible, s, -jnp.inf)
        top = jnp.maximum(jnp.max(s, axis=1, keepdims=True), -1e30)
        probs = jnp.exp(s - top).astype(BF)
        v = kv[:, width + h * HD : width + (h + 1) * HD]
        both = jnp.dot(probs, jnp.concatenate([v, ones], axis=1), preferred_element_type=F32)
        out[:, cols] = both[:, :HD].astype(BF)
        tops.append(top)
        totals.append(both[:, HD : HD + 1])
    out[:, width:] = pack_meta(tops, totals)


def project_kernel(got, w_out, out):
    width = w_out.shape[0]
    parts = []
    for h in range(width // HD):
        top, total = read_meta(got[:, :, width:], h)
        scale = jnp.exp(top - jnp.max(top, axis=0, keepdims=True))
        o = jnp.sum(scale * got[:, :, h * HD : (h + 1) * HD].astype(F32), axis=0)
        parts.append((o / jnp.sum(scale * total, axis=0)).astype(BF))
    projected = jnp.dot(jnp.concatenate(parts, axis=1), w_out[...], preferred_element_type=F32)
    cols = out.shape[2]
    for d in range(out.shape[0]):
        out[d] = projected[:, d * cols : (d + 1) * cols]


def call(kernel, shapes, n_in, smem_first):
    vmem = pl.BlockSpec(memory_space=pltpu.VMEM)
    specs = [vmem] * n_in
    if smem_first:
        specs[0] = pl.BlockSpec(memory_space=pltpu.SMEM)
    return pl.pallas_call(
        kernel,
        out_shape=shapes,
        in_specs=specs,
        out_specs=jax.tree.map(lambda _: vmem, shapes),
        compiler_params=pltpu.CompilerParams(vmem_limit_bytes=LIMIT),
    )


def on_device(latents, context, lengths, w_query, w_key, w_value, w_out):
    lat_dev = latents.shape[0]
    groups = lax.axis_size("ctx")
    heads_axis = lax.axis_size("head")
    width = w_query.shape[1]
    ctx_dev = context.shape[0]
    chips = groups // CORES
    half = chips * lat_dev
    qscale = 1.0 / HD**0.5
    me = lax.axis_index("ctx")
    place = jnp.stack([me % CORES, (me // CORES) * (CORES * ctx_dev)]).astype(jnp.int32)
    same_core = [[c + CORES * g for g in range(chips)] for c in range(CORES)]
    core_pairs = [[CORES * g + c for c in range(CORES)] for g in range(chips)]

    copies = call(
        copies_kernel, jax.ShapeDtypeStruct((heads_axis,) + context.shape, BF), 1, False
    )(context)
    x = lax.all_to_all(copies, "head", 0, 0)

    q = (jnp.dot(latents, w_query, preferred_element_type=F32) * qscale).astype(BF)
    last = min(LAST, chips)
    bit = CORES
    while bit < groups // last:
        pairs = [[i, i | bit] for i in range(groups) if not i & bit]
        q = lax.all_gather(q, "ctx", axis=0, tiled=True, axis_index_groups=pairs)
        bit *= 2
    far = [[i + bit * j for j in range(last)] for i in range(bit)]
    q = lax.all_to_all(
        jnp.broadcast_to(q[None], (last,) + q.shape), "ctx", 0, 0, axis_index_groups=far
    ).reshape(half, width)
    lens = lengths.reshape(chips, CORES, lat_dev).transpose(1, 0, 2).reshape(CORES, half, 1)

    kv = call(key_value_kernel, jax.ShapeDtypeStruct((ctx_dev, 2 * width), BF), 3, False)(
        x, w_key, w_value
    )
    kv = lax.all_gather(kv, "ctx", axis=0, tiled=True, axis_index_groups=core_pairs)
    paired = call(attend_kernel, jax.ShapeDtypeStruct((half, width + META), BF), 4, True)(
        place, kv, q, lens
    )
    got = lax.all_to_all(
        paired.reshape(chips, lat_dev, width + META), "ctx", 0, 0, axis_index_groups=same_core
    )
    cols_dev = w_out.shape[1] // heads_axis
    shares = call(
        project_kernel, jax.ShapeDtypeStruct((heads_axis, lat_dev, cols_dev), F32), 2, False
    )(got, w_out)
    summed = jnp.sum(lax.all_to_all(shares, "head", 0, 0), axis=0)
    first_col = lax.axis_index("head") * cols_dev
    residual = lax.dynamic_slice_in_dim(latents, first_col, cols_dev, 1).astype(F32)
    return (residual + summed).astype(BF)


def solution(mesh):
    in_specs = (
        P("ctx", None),
        P("ctx", "head"),
        P(),
        P(None, "head"),
        P(None, "head"),
        P(None, "head"),
        P("head", None),
    )
    return jax.shard_map(
        on_device, mesh=mesh, in_specs=in_specs, out_specs=P("ctx", "head"), check_vma=False
    )
```

```python
import jax
import jax.numpy as jnp
from jax import lax
from jax.experimental import pallas as pl
from jax.experimental.pallas import tpu as pltpu
from jax.sharding import PartitionSpec as P

HD = 128
META = 128
CORES = 2
FAR = (4, 3, 1, 2, 0)
BF = jnp.bfloat16
F32 = jnp.float32
LIMIT = 40 * 1024 * 1024


def split3(a):
    hi = a.astype(BF).astype(F32)
    rest = a - hi
    mid = rest.astype(BF).astype(F32)
    return [hi, mid, (rest - mid).astype(BF).astype(F32)]


def pack_meta(tops, totals):
    rows = tops[0].shape[0]
    lane = lax.broadcasted_iota(jnp.int32, (rows, META), 1)
    meta = jnp.zeros((rows, META), F32)
    column = 0
    for top, total in zip(tops, totals):
        for part in split3(top) + split3(total):
            meta = jnp.where(lane == column, part, meta)
            column += 1
    return meta.astype(BF)


def read_meta(meta, head):
    m = meta.astype(F32)
    part = [m[..., 6 * head + i : 6 * head + i + 1] for i in range(6)]
    return part[0] + (part[1] + part[2]), part[3] + (part[4] + part[5])


def copies_kernel(context, out, sems):
    copies = [pltpu.make_async_copy(context, out.at[d], sems.at[d]) for d in range(out.shape[0])]
    for copy in copies:
        copy.start()
    for copy in copies:
        copy.wait()


def key_value_kernel(x, wk, wv_hbm, out, wv, sem):
    width = wk.shape[1]
    fetch = pltpu.make_async_copy(wv_hbm, wv, sem)
    fetch.start()
    feats = jnp.concatenate([x[f] for f in range(x.shape[0])], axis=1)
    out[:, :width] = jnp.dot(feats, wk[...], preferred_element_type=F32).astype(BF)
    fetch.wait()
    out[:, width:] = jnp.dot(feats, wv[...], preferred_element_type=F32).astype(BF)


def attend_kernel(place, kv, q, lens, out):
    core, base = place[0], place[1]
    rows, width = q.shape
    positions = kv.shape[0]
    ones = jnp.ones((positions, HD), BF)
    pos = base + lax.broadcasted_iota(jnp.int32, (rows, positions), 1)
    visible = pos < lens[core]
    tops, totals = [], []
    for h in range(width // HD):
        cols = slice(h * HD, (h + 1) * HD)
        s = lax.dot_general(
            q[:, cols], kv[:, cols], (((1,), (1,)), ((), ())), preferred_element_type=F32
        )
        s = jnp.where(visible, s, -jnp.inf)
        top = jnp.maximum(jnp.max(s, axis=1, keepdims=True), -1e30)
        probs = jnp.exp(s - top).astype(BF)
        v = kv[:, width + h * HD : width + (h + 1) * HD]
        both = jnp.dot(probs, jnp.concatenate([v, ones], axis=1), preferred_element_type=F32)
        out[:, cols] = both[:, :HD].astype(BF)
        tops.append(top)
        totals.append(both[:, HD : HD + 1])
    out[:, width:] = pack_meta(tops, totals)


def project_kernel(got, w_out, out):
    width = w_out.shape[0]
    parts = []
    for h in range(width // HD):
        top, total = read_meta(got[:, :, width:], h)
        scale = jnp.exp(top - jnp.max(top, axis=0, keepdims=True))
        o = jnp.sum(scale * got[:, :, h * HD : (h + 1) * HD].astype(F32), axis=0)
        parts.append((o / jnp.sum(scale * total, axis=0)).astype(BF))
    projected = jnp.dot(jnp.concatenate(parts, axis=1), w_out[...], preferred_element_type=F32)
    cols = out.shape[2]
    for d in range(out.shape[0]):
        out[d] = projected[:, d * cols : (d + 1) * cols]


def finish_kernel(place, shares, latents, out):
    cols = out.shape[1]
    first = pl.multiple_of(place[2] * cols, cols)
    summed = jnp.sum(shares[...], axis=0)
    out[...] = (latents[:, pl.ds(first, cols)].astype(F32) + summed).astype(BF)


VMEM = pl.BlockSpec(memory_space=pltpu.VMEM)
SMEM = pl.BlockSpec(memory_space=pltpu.SMEM)
HBM = pl.BlockSpec(memory_space=pltpu.HBM)


def call(kernel, shape, dtype, in_specs, out_spec=VMEM, scratch=()):
    return pl.pallas_call(
        kernel,
        out_shape=jax.ShapeDtypeStruct(shape, dtype),
        in_specs=in_specs,
        out_specs=out_spec,
        scratch_shapes=scratch,
        compiler_params=pltpu.CompilerParams(vmem_limit_bytes=LIMIT),
    )


def on_device(latents, context, lengths, w_query, w_key, w_value, w_out):
    lat_dev = latents.shape[0]
    groups = lax.axis_size("ctx")
    heads_axis = lax.axis_size("head")
    width = w_query.shape[1]
    ctx_dev = context.shape[0]
    chips = groups // CORES
    half = chips * lat_dev
    qscale = 1.0 / HD**0.5
    me = lax.axis_index("ctx")
    my_head = lax.axis_index("head")
    place = jnp.stack([me % CORES, (me // CORES) * (CORES * ctx_dev), my_head]).astype(jnp.int32)

    copies = call(
        copies_kernel,
        (heads_axis,) + context.shape,
        BF,
        [HBM],
        HBM,
        [pltpu.SemaphoreType.DMA((heads_axis,))],
    )(pltpu.with_memory_space_constraint(context, pltpu.HBM))
    x = lax.all_to_all(copies, "head", 0, 0)

    q = (jnp.dot(latents, w_query, preferred_element_type=F32) * qscale).astype(BF)
    bits = chips.bit_length() - 1
    order = sorted(range(bits), key=FAR.index)
    places = [0]
    for b in order:
        step = CORES << b
        pairs = [[i, i | step] for i in range(groups) if not i & step]
        q = lax.all_gather(q, "ctx", axis=0, tiled=True, axis_index_groups=pairs)
        places = places + [p | step for p in places]
    same_core = [[c + p for p in places] for c in range(CORES)]
    core_pairs = [[CORES * g + c for c in range(CORES)] for g in range(chips)]
    lens = lengths.reshape((2,) * bits + (CORES, lat_dev))
    lens = lens.transpose([bits] + [bits - 1 - b for b in reversed(order)] + [bits + 1])
    lens = lens.reshape(CORES, half, 1)

    kv = call(
        key_value_kernel,
        (ctx_dev, 2 * width),
        BF,
        [VMEM, VMEM, HBM],
        VMEM,
        [pltpu.VMEM(w_value.shape, BF), pltpu.SemaphoreType.DMA],
    )(x, w_key, pltpu.with_memory_space_constraint(w_value, pltpu.HBM))
    kv = lax.all_gather(kv, "ctx", axis=0, tiled=True, axis_index_groups=core_pairs)
    part = call(attend_kernel, (half, width + META), BF, [SMEM, VMEM, VMEM, VMEM])(
        place, kv, q, lens
    )
    got = lax.all_to_all(
        part.reshape(chips, lat_dev, width + META), "ctx", 0, 0, axis_index_groups=same_core
    )
    cols_dev = w_out.shape[1] // heads_axis
    shares = call(project_kernel, (heads_axis, lat_dev, cols_dev), F32, [VMEM, VMEM])(got, w_out)
    shares = lax.all_to_all(shares, "head", 0, 0)
    return call(finish_kernel, (lat_dev, cols_dev), BF, [SMEM, VMEM, VMEM])(
        place, shares, latents
    )


def solution(mesh):
    in_specs = (
        P("ctx", None),
        P("ctx", "head"),
        P(),
        P(None, "head"),
        P(None, "head"),
        P(None, "head"),
        P("head", None),
    )
    return jax.shard_map(
        on_device, mesh=mesh, in_specs=in_specs, out_specs=P("ctx", "head"), check_vma=False
    )
```

```python
import jax
import jax.numpy as jnp
from jax import lax
from jax.experimental import pallas as pl
from jax.experimental.pallas import tpu as pltpu
from jax.sharding import PartitionSpec as P

HD = 128
META = 128
CORES = 2
FAR = (4, 3, 1, 2, 0)
BF = jnp.bfloat16
F32 = jnp.float32
LIMIT = 40 * 1024 * 1024


def split3(a):
    hi = a.astype(BF).astype(F32)
    rest = a - hi
    mid = rest.astype(BF).astype(F32)
    return [hi, mid, (rest - mid).astype(BF).astype(F32)]


def pack_meta(tops, totals):
    rows = tops[0].shape[0]
    lane = lax.broadcasted_iota(jnp.int32, (rows, META), 1)
    meta = jnp.zeros((rows, META), F32)
    column = 0
    for top, total in zip(tops, totals):
        for part in split3(top) + split3(total):
            meta = jnp.where(lane == column, part, meta)
            column += 1
    return meta.astype(BF)


def read_meta(meta, head):
    m = meta.astype(F32)
    part = [m[..., 6 * head + i : 6 * head + i + 1] for i in range(6)]
    return part[0] + (part[1] + part[2]), part[3] + (part[4] + part[5])


def copies_kernel(context, out, held, sem, sems):
    fetch = pltpu.make_async_copy(context, held, sem)
    fetch.start()
    fetch.wait()
    copies = [pltpu.make_async_copy(held, out.at[d], sems.at[d]) for d in range(out.shape[0])]
    for copy in copies:
        copy.start()
    for copy in copies:
        copy.wait()


def key_value_kernel(x, wk, wv_hbm, out, wv, sem):
    width = wk.shape[1]
    fetch = pltpu.make_async_copy(wv_hbm, wv, sem)
    fetch.start()
    feats = jnp.concatenate([x[f] for f in range(x.shape[0])], axis=1)
    out[:, :width] = jnp.dot(feats, wk[...], preferred_element_type=F32).astype(BF)
    fetch.wait()
    out[:, width:] = jnp.dot(feats, wv[...], preferred_element_type=F32).astype(BF)


def attend_kernel(place, kv, q, lens, out):
    core, base = place[0], place[1]
    rows, width = q.shape
    positions = kv.shape[0]
    ones = jnp.ones((positions, HD), BF)
    pos = base + lax.broadcasted_iota(jnp.int32, (rows, positions), 1)
    visible = pos < lens[core]
    tops, totals = [], []
    for h in range(width // HD):
        cols = slice(h * HD, (h + 1) * HD)
        s = lax.dot_general(
            q[:, cols], kv[:, cols], (((1,), (1,)), ((), ())), preferred_element_type=F32
        )
        s = jnp.where(visible, s, -jnp.inf)
        top = jnp.maximum(jnp.max(s, axis=1, keepdims=True), -1e30)
        probs = jnp.exp(s - top).astype(BF)
        v = kv[:, width + h * HD : width + (h + 1) * HD]
        both = jnp.dot(probs, jnp.concatenate([v, ones], axis=1), preferred_element_type=F32)
        out[:, cols] = both[:, :HD].astype(BF)
        tops.append(top)
        totals.append(both[:, HD : HD + 1])
    out[:, width:] = pack_meta(tops, totals)


def project_kernel(got, w_out, out):
    width = w_out.shape[0]
    parts = []
    for h in range(width // HD):
        top, total = read_meta(got[:, :, width:], h)
        scale = jnp.exp(top - jnp.max(top, axis=0, keepdims=True))
        o = jnp.sum(scale * got[:, :, h * HD : (h + 1) * HD].astype(F32), axis=0)
        parts.append((o / jnp.sum(scale * total, axis=0)).astype(BF))
    projected = jnp.dot(jnp.concatenate(parts, axis=1), w_out[...], preferred_element_type=F32)
    cols = out.shape[2]
    for d in range(out.shape[0]):
        out[d] = projected[:, d * cols : (d + 1) * cols]


def finish_kernel(place, shares, latents, out):
    cols = out.shape[1]
    first = pl.multiple_of(place[2] * cols, cols)
    summed = jnp.sum(shares[...], axis=0)
    out[...] = (latents[:, pl.ds(first, cols)].astype(F32) + summed).astype(BF)


VMEM = pl.BlockSpec(memory_space=pltpu.VMEM)
SMEM = pl.BlockSpec(memory_space=pltpu.SMEM)
HBM = pl.BlockSpec(memory_space=pltpu.HBM)


def call(kernel, shape, dtype, in_specs, out_spec=VMEM, scratch=()):
    return pl.pallas_call(
        kernel,
        out_shape=jax.ShapeDtypeStruct(shape, dtype),
        in_specs=in_specs,
        out_specs=out_spec,
        scratch_shapes=scratch,
        compiler_params=pltpu.CompilerParams(vmem_limit_bytes=LIMIT),
    )


def on_device(latents, context, lengths, w_query, w_key, w_value, w_out):
    lat_dev = latents.shape[0]
    groups = lax.axis_size("ctx")
    heads_axis = lax.axis_size("head")
    width = w_query.shape[1]
    ctx_dev = context.shape[0]
    chips = groups // CORES
    half = chips * lat_dev
    qscale = 1.0 / HD**0.5
    me = lax.axis_index("ctx")
    my_head = lax.axis_index("head")
    place = jnp.stack([me % CORES, (me // CORES) * (CORES * ctx_dev), my_head]).astype(jnp.int32)

    copies = call(
        copies_kernel,
        (heads_axis,) + context.shape,
        BF,
        [HBM],
        HBM,
        [
            pltpu.VMEM(context.shape, BF),
            pltpu.SemaphoreType.DMA,
            pltpu.SemaphoreType.DMA((heads_axis,)),
        ],
    )(pltpu.with_memory_space_constraint(context, pltpu.HBM))
    x = lax.all_to_all(copies, "head", 0, 0)

    q = (jnp.dot(latents, w_query, preferred_element_type=F32) * qscale).astype(BF)
    bits = chips.bit_length() - 1
    order = sorted(range(bits), key=FAR.index)
    places = [0]
    for b in order:
        step = CORES << b
        pairs = [[i, i | step] for i in range(groups) if not i & step]
        q = lax.all_gather(q, "ctx", axis=0, tiled=True, axis_index_groups=pairs)
        places = places + [p | step for p in places]
    same_core = [[c + p for p in places] for c in range(CORES)]
    core_pairs = [[CORES * g + c for c in range(CORES)] for g in range(chips)]
    lens = lengths.reshape((2,) * bits + (CORES, lat_dev))
    lens = lens.transpose([bits] + [bits - 1 - b for b in reversed(order)] + [bits + 1])
    lens = lens.reshape(CORES, half, 1)

    kv = call(
        key_value_kernel,
        (ctx_dev, 2 * width),
        BF,
        [VMEM, VMEM, HBM],
        VMEM,
        [pltpu.VMEM(w_value.shape, BF), pltpu.SemaphoreType.DMA],
    )(x, w_key, pltpu.with_memory_space_constraint(w_value, pltpu.HBM))
    kv = lax.all_gather(kv, "ctx", axis=0, tiled=True, axis_index_groups=core_pairs)
    part = call(attend_kernel, (half, width + META), BF, [SMEM, VMEM, VMEM, VMEM])(
        place, kv, q, lens
    )
    got = lax.all_to_all(
        part.reshape(chips, lat_dev, width + META), "ctx", 0, 0, axis_index_groups=same_core
    )
    cols_dev = w_out.shape[1] // heads_axis
    shares = call(project_kernel, (heads_axis, lat_dev, cols_dev), F32, [VMEM, VMEM])(got, w_out)
    shares = lax.all_to_all(shares, "head", 0, 0)
    return call(finish_kernel, (lat_dev, cols_dev), BF, [SMEM, VMEM, VMEM])(
        place, shares, latents
    )


def solution(mesh):
    in_specs = (
        P("ctx", None),
        P("ctx", "head"),
        P(),
        P(None, "head"),
        P(None, "head"),
        P(None, "head"),
        P("head", None),
    )
    return jax.shard_map(
        on_device, mesh=mesh, in_specs=in_specs, out_specs=P("ctx", "head"), check_vma=False
    )
```

```python
import functools

import jax
import jax.numpy as jnp
from jax import lax
from jax.experimental import pallas as pl
from jax.experimental.pallas import tpu as pltpu
from jax.sharding import PartitionSpec as P

HD = 128
META = 128
CORES = 2
WV_PARTS = 2
COPY_PARTS = 2
MASKS = (24, 8, 4, 1, 3)
LAST_BIT = 2
BF = jnp.bfloat16
F32 = jnp.float32
LIMIT = 40 * 1024 * 1024


def split3(a):
    hi = a.astype(BF).astype(F32)
    rest = a - hi
    mid = rest.astype(BF).astype(F32)
    return [hi, mid, (rest - mid).astype(BF).astype(F32)]


def pack_meta(tops, totals):
    rows = tops[0].shape[0]
    lane = lax.broadcasted_iota(jnp.int32, (rows, META), 1)
    meta = jnp.zeros((rows, META), F32)
    column = 0
    for top, total in zip(tops, totals):
        for part in split3(top) + split3(total):
            meta = jnp.where(lane == column, part, meta)
            column += 1
    return meta.astype(BF)


def read_meta(meta, head):
    m = meta.astype(F32)
    part = [m[..., 6 * head + i : 6 * head + i + 1] for i in range(6)]
    return part[0] + (part[1] + part[2]), part[3] + (part[4] + part[5])


def copies_kernel(context, out, held, sems, out_sems):
    parts = sems.shape[0]
    step = held.shape[0] // parts
    rows = [pl.ds(i * step, step) for i in range(parts)]
    fetches = [
        pltpu.make_async_copy(context.at[r], held.at[r], sems.at[i]) for i, r in enumerate(rows)
    ]
    for fetch in fetches:
        fetch.start()
    sends = []
    for i, r in enumerate(rows):
        fetches[i].wait()
        for d in range(out.shape[0]):
            send = pltpu.make_async_copy(held.at[r], out.at[d, r], out_sems.at[i, d])
            send.start()
            sends.append(send)
    for send in sends:
        send.wait()


def key_value_kernel(x, wk, wv_hbm, out, wv, sems):
    width = wk.shape[1]
    step = wv.shape[0] // WV_PARTS
    parts = [pl.ds(i * step, step) for i in range(WV_PARTS)]
    fetches = [
        pltpu.make_async_copy(wv_hbm.at[part], wv.at[part], sems.at[i])
        for i, part in enumerate(parts)
    ]
    for fetch in fetches:
        fetch.start()
    feats = jnp.concatenate([x[f] for f in range(x.shape[0])], axis=1)
    out[:, :width] = jnp.dot(feats, wk[...], preferred_element_type=F32).astype(BF)
    for fetch in fetches:
        fetch.wait()
    out[:, width:] = jnp.dot(feats, wv[...], preferred_element_type=F32).astype(BF)


def attend_kernel(spots, bit, kv, q_own, q_got, lens, out):
    me = lax.axis_index("ctx")
    width = q_own.shape[1]
    positions = kv.shape[0]
    core, base = me % CORES, (me // CORES) * positions
    lower = (me // bit) % 2 == 0
    own, other = q_own[...], q_got[...]
    q = jnp.concatenate([jnp.where(lower, own, other), jnp.where(lower, other, own)], axis=0)
    rows = q.shape[0]
    step = rows // len(spots)
    natural = lens[core]
    last = jnp.concatenate([natural[p * step : (p + 1) * step] for p in spots], axis=0)
    visible = base + lax.broadcasted_iota(jnp.int32, (rows, positions), 1) < last
    ones = jnp.ones((positions, HD), BF)
    tops, totals = [], []
    for h in range(width // HD):
        cols = slice(h * HD, (h + 1) * HD)
        s = lax.dot_general(
            q[:, cols], kv[:, cols], (((1,), (1,)), ((), ())), preferred_element_type=F32
        )
        s = jnp.where(visible, s, -jnp.inf)
        top = jnp.maximum(jnp.max(s, axis=1, keepdims=True), -1e30)
        probs = jnp.exp(s - top).astype(BF)
        v = kv[:, width + h * HD : width + (h + 1) * HD]
        both = jnp.dot(probs, jnp.concatenate([v, ones], axis=1), preferred_element_type=F32)
        out[:, cols] = both[:, :HD].astype(BF)
        tops.append(top)
        totals.append(both[:, HD : HD + 1])
    out[:, width:] = pack_meta(tops, totals)


def project_kernel(got, w_out, latents, out):
    width = w_out.shape[0]
    parts = []
    for h in range(width // HD):
        top, total = read_meta(got[:, :, width:], h)
        scale = jnp.exp(top - jnp.max(top, axis=0, keepdims=True))
        o = jnp.sum(scale * got[:, :, h * HD : (h + 1) * HD].astype(F32), axis=0)
        parts.append((o / jnp.sum(scale * total, axis=0)).astype(BF))
    projected = jnp.dot(jnp.concatenate(parts, axis=1), w_out[...], preferred_element_type=F32)
    cols = out.shape[2]
    for d in range(out.shape[0]):
        out[d] = projected[:, d * cols : (d + 1) * cols]
    mine = lax.axis_index("head")
    first = pl.multiple_of(mine * cols, cols)
    out[mine] = out[mine] + latents[:, pl.ds(first, cols)].astype(F32)


def finish_kernel(shares, out):
    out[...] = jnp.sum(shares[...], axis=0).astype(BF)


VMEM = pl.BlockSpec(memory_space=pltpu.VMEM)
HBM = pl.BlockSpec(memory_space=pltpu.HBM)


def call(kernel, out_shape, in_specs, out_specs=VMEM, scratch=()):
    return pl.pallas_call(
        kernel,
        out_shape=out_shape,
        in_specs=in_specs,
        out_specs=out_specs,
        scratch_shapes=scratch,
        compiler_params=pltpu.CompilerParams(vmem_limit_bytes=LIMIT),
    )


def in_hbm(a):
    return pltpu.with_memory_space_constraint(a, pltpu.HBM)


def on_device(latents, context, lengths, w_query, w_key, w_value, w_out):
    lat_dev = latents.shape[0]
    groups = lax.axis_size("ctx")
    heads_axis = lax.axis_size("head")
    width = w_query.shape[1]
    ctx_dev = context.shape[0]
    chips = groups // CORES
    half = chips * lat_dev
    copies = call(
        copies_kernel,
        jax.ShapeDtypeStruct((heads_axis,) + context.shape, BF),
        [HBM],
        HBM,
        [
            pltpu.VMEM(context.shape, BF),
            pltpu.SemaphoreType.DMA((COPY_PARTS,)),
            pltpu.SemaphoreType.DMA((COPY_PARTS, heads_axis)),
        ],
    )(in_hbm(context))
    x = lax.all_to_all(copies, "head", 0, 0)

    qscale = 1.0 / HD**0.5
    q = (jnp.dot(latents, w_query, preferred_element_type=F32) * qscale).astype(BF)

    masks = [CORES * m for m in MASKS]
    held = [[i] for i in range(groups)]
    for step, mask in enumerate(masks):
        pairs = [
            [i, i ^ mask] for i in range(groups) if min(held[i]) < min(held[i ^ mask])
        ]
        if step < len(masks) - 1:
            q = lax.all_gather(q, "ctx", axis=0, tiled=True, axis_index_groups=pairs)
        for i, j in pairs:
            held[i] = held[j] = held[i] + held[j]
    q_got = lax.ppermute(q, "ctx", [(i, i ^ masks[-1]) for i in range(groups)])
    same_core = [held[c] for c in range(CORES)]
    spots = [d // CORES for d in held[0]]
    core_pairs = [[CORES * g + c for c in range(CORES)] for g in range(chips)]
    lens = lengths.reshape(chips, CORES, lat_dev).transpose(1, 0, 2).reshape(CORES, half, 1)

    kv = call(
        key_value_kernel,
        jax.ShapeDtypeStruct((ctx_dev, 2 * width), BF),
        [VMEM, VMEM, HBM],
        VMEM,
        [pltpu.VMEM(w_value.shape, BF), pltpu.SemaphoreType.DMA((WV_PARTS,))],
    )(x, w_key, in_hbm(w_value))
    kv = lax.all_gather(kv, "ctx", axis=0, tiled=True, axis_index_groups=core_pairs)
    part = call(
        functools.partial(attend_kernel, spots, CORES * LAST_BIT),
        jax.ShapeDtypeStruct((half, width + META), BF),
        [VMEM, VMEM, VMEM, VMEM],
    )(kv, q, q_got, lens)
    got = lax.all_to_all(
        part.reshape(chips, lat_dev, width + META), "ctx", 0, 0, axis_index_groups=same_core
    )
    cols_dev = w_out.shape[1] // heads_axis
    shares = call(
        project_kernel,
        jax.ShapeDtypeStruct((heads_axis, lat_dev, cols_dev), F32),
        [VMEM, VMEM, VMEM],
    )(got, w_out, latents)
    shares = lax.all_to_all(shares, "head", 0, 0)
    return call(finish_kernel, jax.ShapeDtypeStruct((lat_dev, cols_dev), BF), [VMEM])(shares)


def solution(mesh):
    in_specs = (
        P("ctx", None),
        P("ctx", "head"),
        P(),
        P(None, "head"),
        P(None, "head"),
        P(None, "head"),
        P("head", None),
    )
    return jax.shard_map(
        on_device, mesh=mesh, in_specs=in_specs, out_specs=P("ctx", "head"), check_vma=False
    )
```

```python
import functools

import jax
import jax.numpy as jnp
from jax import lax
from jax.experimental import pallas as pl
from jax.experimental.pallas import tpu as pltpu
from jax.sharding import PartitionSpec as P

HD = 128
META = 128
CORES = 2
WV_PARTS = 2
COPY_PARTS = 2
MASKS = (24, 8, 4, 1, 3)
LAST_BIT = 2
BF = jnp.bfloat16
F32 = jnp.float32
LIMIT = 40 * 1024 * 1024


def split3(a):
    hi = a.astype(BF).astype(F32)
    rest = a - hi
    mid = rest.astype(BF).astype(F32)
    return [hi, mid, (rest - mid).astype(BF).astype(F32)]


def pack_meta(tops, totals):
    rows = tops[0].shape[0]
    lane = lax.broadcasted_iota(jnp.int32, (rows, META), 1)
    meta = jnp.zeros((rows, META), F32)
    column = 0
    for top, total in zip(tops, totals):
        for part in split3(top) + split3(total):
            meta = jnp.where(lane == column, part, meta)
            column += 1
    return meta.astype(BF)


def read_meta(meta, head):
    m = meta.astype(F32)
    part = [m[..., 6 * head + i : 6 * head + i + 1] for i in range(6)]
    return part[0] + (part[1] + part[2]), part[3] + (part[4] + part[5])


def copies_kernel(context, out, held, sems, out_sems):
    parts = sems.shape[0]
    step = held.shape[0] // parts
    rows = [pl.ds(i * step, step) for i in range(parts)]
    fetches = [
        pltpu.make_async_copy(context.at[r], held.at[r], sems.at[i]) for i, r in enumerate(rows)
    ]
    for fetch in fetches:
        fetch.start()
    sends = []
    for i, r in enumerate(rows):
        fetches[i].wait()
        for d in range(out.shape[0]):
            send = pltpu.make_async_copy(held.at[r], out.at[d, r], out_sems.at[i, d])
            send.start()
            sends.append(send)
    for send in sends:
        send.wait()


def key_value_kernel(x, wk, wv_hbm, out, wv, sems):
    width = wk.shape[1]
    step = wv.shape[0] // WV_PARTS
    parts = [pl.ds(i * step, step) for i in range(WV_PARTS)]
    fetches = [
        pltpu.make_async_copy(wv_hbm.at[part], wv.at[part], sems.at[i])
        for i, part in enumerate(parts)
    ]
    for fetch in fetches:
        fetch.start()
    feats = jnp.concatenate([x[f] for f in range(x.shape[0])], axis=1)
    out[:, :width] = jnp.dot(feats, wk[...], preferred_element_type=F32).astype(BF)
    for fetch in fetches:
        fetch.wait()
    out[:, width:] = jnp.dot(feats, wv[...], preferred_element_type=F32).astype(BF)


def attend_kernel(spots, bit, kv, q_own, q_got, lens, out):
    me = lax.axis_index("ctx")
    width = q_own.shape[1]
    positions = kv.shape[0]
    core, base = me % CORES, (me // CORES) * positions
    lower = (me // bit) % 2 == 0
    own, other = q_own[...], q_got[...]
    q = jnp.concatenate([jnp.where(lower, own, other), jnp.where(lower, other, own)], axis=0)
    rows = q.shape[0]
    step = rows // len(spots)
    column = jnp.broadcast_to(lens[...].astype(F32), (8, lens.shape[1])).T[:, :1]
    tiles = [column[i * step : (i + 1) * step] for i in range(CORES * len(spots))]
    last = jnp.concatenate(
        [jnp.where(core == 0, tiles[CORES * p], tiles[CORES * p + 1]) for p in spots], axis=0
    ).astype(jnp.int32)
    visible = base + lax.broadcasted_iota(jnp.int32, (rows, positions), 1) < last
    ones = jnp.ones((positions, HD), BF)
    tops, totals = [], []
    for h in range(width // HD):
        cols = slice(h * HD, (h + 1) * HD)
        s = lax.dot_general(
            q[:, cols], kv[:, cols], (((1,), (1,)), ((), ())), preferred_element_type=F32
        )
        s = jnp.where(visible, s, -jnp.inf)
        top = jnp.maximum(jnp.max(s, axis=1, keepdims=True), -1e30)
        probs = jnp.exp(s - top).astype(BF)
        v = kv[:, width + h * HD : width + (h + 1) * HD]
        both = jnp.dot(probs, jnp.concatenate([v, ones], axis=1), preferred_element_type=F32)
        out[:, cols] = both[:, :HD].astype(BF)
        tops.append(top)
        totals.append(both[:, HD : HD + 1])
    out[:, width:] = pack_meta(tops, totals)


def project_kernel(got, w_out, latents, out):
    width = w_out.shape[0]
    parts = []
    for h in range(width // HD):
        top, total = read_meta(got[:, :, width:], h)
        scale = jnp.exp(top - jnp.max(top, axis=0, keepdims=True))
        o = jnp.sum(scale * got[:, :, h * HD : (h + 1) * HD].astype(F32), axis=0)
        parts.append((o / jnp.sum(scale * total, axis=0)).astype(BF))
    projected = jnp.dot(jnp.concatenate(parts, axis=1), w_out[...], preferred_element_type=F32)
    cols = out.shape[2]
    for d in range(out.shape[0]):
        out[d] = projected[:, d * cols : (d + 1) * cols]
    mine = lax.axis_index("head")
    first = pl.multiple_of(mine * cols, cols)
    out[mine] = out[mine] + latents[:, pl.ds(first, cols)].astype(F32)


def finish_kernel(shares, out):
    out[...] = jnp.sum(shares[...], axis=0).astype(BF)


VMEM = pl.BlockSpec(memory_space=pltpu.VMEM)
HBM = pl.BlockSpec(memory_space=pltpu.HBM)


def call(kernel, out_shape, in_specs, out_specs=VMEM, scratch=()):
    return pl.pallas_call(
        kernel,
        out_shape=out_shape,
        in_specs=in_specs,
        out_specs=out_specs,
        scratch_shapes=scratch,
        compiler_params=pltpu.CompilerParams(vmem_limit_bytes=LIMIT),
    )


def in_hbm(a):
    return pltpu.with_memory_space_constraint(a, pltpu.HBM)


def on_device(latents, context, lengths, w_query, w_key, w_value, w_out):
    lat_dev = latents.shape[0]
    groups = lax.axis_size("ctx")
    heads_axis = lax.axis_size("head")
    width = w_query.shape[1]
    ctx_dev = context.shape[0]
    chips = groups // CORES
    half = chips * lat_dev
    copies = call(
        copies_kernel,
        jax.ShapeDtypeStruct((heads_axis,) + context.shape, BF),
        [HBM],
        HBM,
        [
            pltpu.VMEM(context.shape, BF),
            pltpu.SemaphoreType.DMA((COPY_PARTS,)),
            pltpu.SemaphoreType.DMA((COPY_PARTS, heads_axis)),
        ],
    )(in_hbm(context))
    x = lax.all_to_all(copies, "head", 0, 0)

    qscale = 1.0 / HD**0.5
    q = (jnp.dot(latents, w_query, preferred_element_type=F32) * qscale).astype(BF)

    masks = [CORES * m for m in MASKS]
    held = [[i] for i in range(groups)]
    for step, mask in enumerate(masks):
        pairs = [
            [i, i ^ mask] for i in range(groups) if min(held[i]) < min(held[i ^ mask])
        ]
        if step < len(masks) - 1:
            q = lax.all_gather(q, "ctx", axis=0, tiled=True, axis_index_groups=pairs)
        for i, j in pairs:
            held[i] = held[j] = held[i] + held[j]
    q_got = lax.ppermute(q, "ctx", [(i, i ^ masks[-1]) for i in range(groups)])
    same_core = [held[c] for c in range(CORES)]
    spots = [d // CORES for d in held[0]]
    core_pairs = [[CORES * g + c for c in range(CORES)] for g in range(chips)]
    kv = call(
        key_value_kernel,
        jax.ShapeDtypeStruct((ctx_dev, 2 * width), BF),
        [VMEM, VMEM, HBM],
        VMEM,
        [pltpu.VMEM(w_value.shape, BF), pltpu.SemaphoreType.DMA((WV_PARTS,))],
    )(x, w_key, in_hbm(w_value))
    kv = lax.all_gather(kv, "ctx", axis=0, tiled=True, axis_index_groups=core_pairs)
    part = call(
        functools.partial(attend_kernel, spots, CORES * LAST_BIT),
        jax.ShapeDtypeStruct((half, width + META), BF),
        [VMEM, VMEM, VMEM, VMEM],
    )(kv, q, q_got, lengths.reshape(1, -1))
    got = lax.all_to_all(
        part.reshape(chips, lat_dev, width + META), "ctx", 0, 0, axis_index_groups=same_core
    )
    cols_dev = w_out.shape[1] // heads_axis
    shares = call(
        project_kernel,
        jax.ShapeDtypeStruct((heads_axis, lat_dev, cols_dev), F32),
        [VMEM, VMEM, VMEM],
    )(got, w_out, latents)
    shares = lax.all_to_all(shares, "head", 0, 0)
    return call(finish_kernel, jax.ShapeDtypeStruct((lat_dev, cols_dev), BF), [VMEM])(shares)


def solution(mesh):
    in_specs = (
        P("ctx", None),
        P("ctx", "head"),
        P(),
        P(None, "head"),
        P(None, "head"),
        P(None, "head"),
        P("head", None),
    )
    return jax.shard_map(
        on_device, mesh=mesh, in_specs=in_specs, out_specs=P("ctx", "head"), check_vma=False
    )
```

```python
import functools

import jax
import jax.numpy as jnp
from jax import lax
from jax.experimental import pallas as pl
from jax.experimental.pallas import tpu as pltpu
from jax.sharding import PartitionSpec as P

HD = 128
META = 128
CORES = 2
WV_PARTS = 2
COPY_PARTS = 2
RING = (0, 1, 4, 5, 3, 2, 7, 6)
MASKS = (24, 8, 4, 1, 3)
LAST_BIT = 2
BF = jnp.bfloat16
F32 = jnp.float32
LIMIT = 40 * 1024 * 1024


def split3(a):
    hi = a.astype(BF).astype(F32)
    rest = a - hi
    mid = rest.astype(BF).astype(F32)
    return [hi, mid, (rest - mid).astype(BF).astype(F32)]


def pack_meta(tops, totals):
    rows = tops[0].shape[0]
    lane = lax.broadcasted_iota(jnp.int32, (rows, META), 1)
    meta = jnp.zeros((rows, META), F32)
    column = 0
    for top, total in zip(tops, totals):
        for part in split3(top) + split3(total):
            meta = jnp.where(lane == column, part, meta)
            column += 1
    return meta.astype(BF)


def read_meta(meta, head):
    m = meta.astype(F32)
    part = [m[..., 6 * head + i : 6 * head + i + 1] for i in range(6)]
    return part[0] + (part[1] + part[2]), part[3] + (part[4] + part[5])


def copies_kernel(context, out, held, sems, out_sems):
    parts = sems.shape[0]
    step = held.shape[0] // parts
    rows = [pl.ds(i * step, step) for i in range(parts)]
    fetches = [
        pltpu.make_async_copy(context.at[r], held.at[r], sems.at[i]) for i, r in enumerate(rows)
    ]
    for fetch in fetches:
        fetch.start()
    sends = []
    for i, r in enumerate(rows):
        fetches[i].wait()
        for d in range(out.shape[0]):
            send = pltpu.make_async_copy(held.at[r], out.at[d, r], out_sems.at[i, d])
            send.start()
            sends.append(send)
    for send in sends:
        send.wait()


def key_value_kernel(x, wk, wv_hbm, out, wv, sems):
    width = wk.shape[1]
    step = wv.shape[0] // WV_PARTS
    parts = [pl.ds(i * step, step) for i in range(WV_PARTS)]
    fetches = [
        pltpu.make_async_copy(wv_hbm.at[part], wv.at[part], sems.at[i])
        for i, part in enumerate(parts)
    ]
    for fetch in fetches:
        fetch.start()
    feats = jnp.concatenate([x[RING.index(f)] for f in range(x.shape[0])], axis=1)
    out[:, :width] = jnp.dot(feats, wk[...], preferred_element_type=F32).astype(BF)
    for fetch in fetches:
        fetch.wait()
    out[:, width:] = jnp.dot(feats, wv[...], preferred_element_type=F32).astype(BF)


def attend_kernel(spots, bit, kv, q_own, q_got, lens, out):
    me = lax.axis_index("ctx")
    width = q_own.shape[1]
    positions = kv.shape[0]
    core, base = me % CORES, (me // CORES) * positions
    lower = (me // bit) % 2 == 0
    own, other = q_own[...], q_got[...]
    q = jnp.concatenate([jnp.where(lower, own, other), jnp.where(lower, other, own)], axis=0)
    rows = q.shape[0]
    step = rows // len(spots)
    column = jnp.broadcast_to(lens[...].astype(F32), (8, lens.shape[1])).T[:, :1]
    tiles = [column[i * step : (i + 1) * step] for i in range(CORES * len(spots))]
    last = jnp.concatenate(
        [jnp.where(core == 0, tiles[CORES * p], tiles[CORES * p + 1]) for p in spots], axis=0
    ).astype(jnp.int32)
    visible = base + lax.broadcasted_iota(jnp.int32, (rows, positions), 1) < last
    ones = jnp.ones((positions, HD), BF)
    tops, totals = [], []
    for h in range(width // HD):
        cols = slice(h * HD, (h + 1) * HD)
        s = lax.dot_general(
            q[:, cols], kv[:, cols], (((1,), (1,)), ((), ())), preferred_element_type=F32
        )
        s = jnp.where(visible, s, -jnp.inf)
        top = jnp.maximum(jnp.max(s, axis=1, keepdims=True), -1e30)
        probs = jnp.exp(s - top).astype(BF)
        v = kv[:, width + h * HD : width + (h + 1) * HD]
        both = jnp.dot(probs, jnp.concatenate([v, ones], axis=1), preferred_element_type=F32)
        out[:, cols] = both[:, :HD].astype(BF)
        tops.append(top)
        totals.append(both[:, HD : HD + 1])
    out[:, width:] = pack_meta(tops, totals)


def project_kernel(got, w_out, latents, out):
    width = w_out.shape[0]
    parts = []
    for h in range(width // HD):
        top, total = read_meta(got[:, :, width:], h)
        scale = jnp.exp(top - jnp.max(top, axis=0, keepdims=True))
        o = jnp.sum(scale * got[:, :, h * HD : (h + 1) * HD].astype(F32), axis=0)
        parts.append((o / jnp.sum(scale * total, axis=0)).astype(BF))
    projected = jnp.dot(jnp.concatenate(parts, axis=1), w_out[...], preferred_element_type=F32)
    cols = out.shape[2]
    for at, d in enumerate(RING):
        out[at] = projected[:, d * cols : (d + 1) * cols]
    head = lax.axis_index("head")
    mine = sum(jnp.where(head == d, at, 0) for at, d in enumerate(RING))
    first = pl.multiple_of(head * cols, cols)
    out[mine] = out[mine] + latents[:, pl.ds(first, cols)].astype(F32)


def finish_kernel(shares, out):
    out[...] = jnp.sum(shares[...], axis=0).astype(BF)


VMEM = pl.BlockSpec(memory_space=pltpu.VMEM)
HBM = pl.BlockSpec(memory_space=pltpu.HBM)


def call(kernel, out_shape, in_specs, out_specs=VMEM, scratch=()):
    return pl.pallas_call(
        kernel,
        out_shape=out_shape,
        in_specs=in_specs,
        out_specs=out_specs,
        scratch_shapes=scratch,
        compiler_params=pltpu.CompilerParams(vmem_limit_bytes=LIMIT),
    )


def in_hbm(a):
    return pltpu.with_memory_space_constraint(a, pltpu.HBM)


def on_device(latents, context, lengths, w_query, w_key, w_value, w_out):
    lat_dev = latents.shape[0]
    groups = lax.axis_size("ctx")
    heads_axis = lax.axis_size("head")
    width = w_query.shape[1]
    ctx_dev = context.shape[0]
    chips = groups // CORES
    half = chips * lat_dev
    copies = call(
        copies_kernel,
        jax.ShapeDtypeStruct((heads_axis,) + context.shape, BF),
        [HBM],
        HBM,
        [
            pltpu.VMEM(context.shape, BF),
            pltpu.SemaphoreType.DMA((COPY_PARTS,)),
            pltpu.SemaphoreType.DMA((COPY_PARTS, heads_axis)),
        ],
    )(in_hbm(context))
    x = lax.all_to_all(copies, "head", 0, 0, axis_index_groups=[RING])

    qscale = 1.0 / HD**0.5
    q = (jnp.dot(latents, w_query, preferred_element_type=F32) * qscale).astype(BF)

    masks = [CORES * m for m in MASKS]
    held = [[i] for i in range(groups)]
    for step, mask in enumerate(masks):
        pairs = [
            [i, i ^ mask] for i in range(groups) if min(held[i]) < min(held[i ^ mask])
        ]
        if step < len(masks) - 1:
            q = lax.all_gather(q, "ctx", axis=0, tiled=True, axis_index_groups=pairs)
        for i, j in pairs:
            held[i] = held[j] = held[i] + held[j]
    q_got = lax.ppermute(q, "ctx", [(i, i ^ masks[-1]) for i in range(groups)])
    same_core = [held[c] for c in range(CORES)]
    spots = [d // CORES for d in held[0]]
    core_pairs = [[CORES * g + c for c in range(CORES)] for g in range(chips)]
    kv = call(
        key_value_kernel,
        jax.ShapeDtypeStruct((ctx_dev, 2 * width), BF),
        [VMEM, VMEM, HBM],
        VMEM,
        [pltpu.VMEM(w_value.shape, BF), pltpu.SemaphoreType.DMA((WV_PARTS,))],
    )(x, w_key, in_hbm(w_value))
    kv = lax.all_gather(kv, "ctx", axis=0, tiled=True, axis_index_groups=core_pairs)
    part = call(
        functools.partial(attend_kernel, spots, CORES * LAST_BIT),
        jax.ShapeDtypeStruct((half, width + META), BF),
        [VMEM, VMEM, VMEM, VMEM],
    )(kv, q, q_got, lengths.reshape(1, -1))
    got = lax.all_to_all(
        part.reshape(chips, lat_dev, width + META), "ctx", 0, 0, axis_index_groups=same_core
    )
    cols_dev = w_out.shape[1] // heads_axis
    shares = call(
        project_kernel,
        jax.ShapeDtypeStruct((heads_axis, lat_dev, cols_dev), F32),
        [VMEM, VMEM, VMEM],
    )(got, w_out, latents)
    shares = lax.all_to_all(shares, "head", 0, 0, axis_index_groups=[RING])
    return call(finish_kernel, jax.ShapeDtypeStruct((lat_dev, cols_dev), BF), [VMEM])(shares)


def solution(mesh):
    in_specs = (
        P("ctx", None),
        P("ctx", "head"),
        P(),
        P(None, "head"),
        P(None, "head"),
        P(None, "head"),
        P("head", None),
    )
    return jax.shard_map(
        on_device, mesh=mesh, in_specs=in_specs, out_specs=P("ctx", "head"), check_vma=False
    )
```

```python
import functools

import jax
import jax.numpy as jnp
from jax import lax
from jax.experimental import pallas as pl
from jax.experimental.pallas import tpu as pltpu
from jax.sharding import PartitionSpec as P

HD = 128
META = 128
CORES = 2
WV_PARTS = 2
COPY_PARTS = 2
RING = (0, 1, 4, 5, 3, 2, 7, 6)
MASKS = (8, 4, 24, 1, 3)
LAST_BIT = 2
BF = jnp.bfloat16
F32 = jnp.float32
LIMIT = 40 * 1024 * 1024


def split3(a):
    hi = a.astype(BF).astype(F32)
    rest = a - hi
    mid = rest.astype(BF).astype(F32)
    return [hi, mid, (rest - mid).astype(BF).astype(F32)]


def pack_meta(tops, totals):
    rows = tops[0].shape[0]
    lane = lax.broadcasted_iota(jnp.int32, (rows, META), 1)
    meta = jnp.zeros((rows, META), F32)
    column = 0
    for top, total in zip(tops, totals):
        for part in split3(top) + split3(total):
            meta = jnp.where(lane == column, part, meta)
            column += 1
    return meta.astype(BF)


def read_meta(meta, head):
    m = meta.astype(F32)
    part = [m[..., 6 * head + i : 6 * head + i + 1] for i in range(6)]
    return part[0] + (part[1] + part[2]), part[3] + (part[4] + part[5])


def copies_kernel(context, out, held, sems, out_sems):
    parts = sems.shape[0]
    step = held.shape[0] // parts
    rows = [pl.ds(i * step, step) for i in range(parts)]
    fetches = [
        pltpu.make_async_copy(context.at[r], held.at[r], sems.at[i]) for i, r in enumerate(rows)
    ]
    for fetch in fetches:
        fetch.start()
    sends = []
    for i, r in enumerate(rows):
        fetches[i].wait()
        for d in range(out.shape[0]):
            send = pltpu.make_async_copy(held.at[r], out.at[d, r], out_sems.at[i, d])
            send.start()
            sends.append(send)
    for send in sends:
        send.wait()


def key_value_kernel(x, wk, wv_hbm, out, wv, sems):
    width = wk.shape[1]
    step = wv.shape[0] // WV_PARTS
    parts = [pl.ds(i * step, step) for i in range(WV_PARTS)]
    fetches = [
        pltpu.make_async_copy(wv_hbm.at[part], wv.at[part], sems.at[i])
        for i, part in enumerate(parts)
    ]
    for fetch in fetches:
        fetch.start()
    feats = jnp.concatenate([x[RING.index(f)] for f in range(x.shape[0])], axis=1)
    out[:, :width] = jnp.dot(feats, wk[...], preferred_element_type=F32).astype(BF)
    for fetch in fetches:
        fetch.wait()
    out[:, width:] = jnp.dot(feats, wv[...], preferred_element_type=F32).astype(BF)


def attend_kernel(spots, bit, kv, q_own, q_got, lens, out):
    me = lax.axis_index("ctx")
    width = q_own.shape[1]
    positions = kv.shape[0]
    core, base = me % CORES, (me // CORES) * positions
    lower = (me // bit) % 2 == 0
    own, other = q_own[...], q_got[...]
    q = jnp.concatenate([jnp.where(lower, own, other), jnp.where(lower, other, own)], axis=0)
    rows = q.shape[0]
    step = rows // len(spots)
    column = jnp.broadcast_to(lens[...].astype(F32), (8, lens.shape[1])).T[:, :1]
    tiles = [column[i * step : (i + 1) * step] for i in range(CORES * len(spots))]
    last = jnp.concatenate(
        [jnp.where(core == 0, tiles[CORES * p], tiles[CORES * p + 1]) for p in spots], axis=0
    ).astype(jnp.int32)
    visible = base + lax.broadcasted_iota(jnp.int32, (rows, positions), 1) < last
    ones = jnp.ones((positions, HD), BF)
    tops, totals = [], []
    for h in range(width // HD):
        cols = slice(h * HD, (h + 1) * HD)
        s = lax.dot_general(
            q[:, cols], kv[:, cols], (((1,), (1,)), ((), ())), preferred_element_type=F32
        )
        s = jnp.where(visible, s, -jnp.inf)
        top = jnp.maximum(jnp.max(s, axis=1, keepdims=True), -1e30)
        probs = jnp.exp(s - top).astype(BF)
        v = kv[:, width + h * HD : width + (h + 1) * HD]
        both = jnp.dot(probs, jnp.concatenate([v, ones], axis=1), preferred_element_type=F32)
        out[:, cols] = both[:, :HD].astype(BF)
        tops.append(top)
        totals.append(both[:, HD : HD + 1])
    out[:, width:] = pack_meta(tops, totals)


def project_kernel(got, w_out, latents, out):
    width = w_out.shape[0]
    parts = []
    for h in range(width // HD):
        top, total = read_meta(got[:, :, width:], h)
        scale = jnp.exp(top - jnp.max(top, axis=0, keepdims=True))
        o = jnp.sum(scale * got[:, :, h * HD : (h + 1) * HD].astype(F32), axis=0)
        parts.append((o / jnp.sum(scale * total, axis=0)).astype(BF))
    projected = jnp.dot(jnp.concatenate(parts, axis=1), w_out[...], preferred_element_type=F32)
    cols = out.shape[2]
    for at, d in enumerate(RING):
        out[at] = projected[:, d * cols : (d + 1) * cols]
    head = lax.axis_index("head")
    mine = sum(jnp.where(head == d, at, 0) for at, d in enumerate(RING))
    first = pl.multiple_of(head * cols, cols)
    out[mine] = out[mine] + latents[:, pl.ds(first, cols)].astype(F32)


def finish_kernel(shares, out):
    out[...] = jnp.sum(shares[...], axis=0).astype(BF)


VMEM = pl.BlockSpec(memory_space=pltpu.VMEM)
HBM = pl.BlockSpec(memory_space=pltpu.HBM)


def call(kernel, out_shape, in_specs, out_specs=VMEM, scratch=()):
    return pl.pallas_call(
        kernel,
        out_shape=out_shape,
        in_specs=in_specs,
        out_specs=out_specs,
        scratch_shapes=scratch,
        compiler_params=pltpu.CompilerParams(vmem_limit_bytes=LIMIT),
    )


def in_hbm(a):
    return pltpu.with_memory_space_constraint(a, pltpu.HBM)


def on_device(latents, context, lengths, w_query, w_key, w_value, w_out):
    lat_dev = latents.shape[0]
    groups = lax.axis_size("ctx")
    heads_axis = lax.axis_size("head")
    width = w_query.shape[1]
    ctx_dev = context.shape[0]
    chips = groups // CORES
    half = chips * lat_dev
    copies = call(
        copies_kernel,
        jax.ShapeDtypeStruct((heads_axis,) + context.shape, BF),
        [HBM],
        HBM,
        [
            pltpu.VMEM(context.shape, BF),
            pltpu.SemaphoreType.DMA((COPY_PARTS,)),
            pltpu.SemaphoreType.DMA((COPY_PARTS, heads_axis)),
        ],
    )(in_hbm(context))
    x = lax.all_to_all(copies, "head", 0, 0, axis_index_groups=[RING])

    qscale = 1.0 / HD**0.5
    q = (jnp.dot(latents, w_query, preferred_element_type=F32) * qscale).astype(BF)

    masks = [CORES * m for m in MASKS]
    held = [[i] for i in range(groups)]
    for step, mask in enumerate(masks):
        pairs = [
            [i, i ^ mask] for i in range(groups) if min(held[i]) < min(held[i ^ mask])
        ]
        if step < len(masks) - 1:
            q = lax.all_gather(q, "ctx", axis=0, tiled=True, axis_index_groups=pairs)
        for i, j in pairs:
            held[i] = held[j] = held[i] + held[j]
    q_got = lax.ppermute(q, "ctx", [(i, i ^ masks[-1]) for i in range(groups)])
    same_core = [held[c] for c in range(CORES)]
    spots = [d // CORES for d in held[0]]
    core_pairs = [[CORES * g + c for c in range(CORES)] for g in range(chips)]
    kv = call(
        key_value_kernel,
        jax.ShapeDtypeStruct((ctx_dev, 2 * width), BF),
        [VMEM, VMEM, HBM],
        VMEM,
        [pltpu.VMEM(w_value.shape, BF), pltpu.SemaphoreType.DMA((WV_PARTS,))],
    )(x, w_key, in_hbm(w_value))
    kv = lax.all_gather(kv, "ctx", axis=0, tiled=True, axis_index_groups=core_pairs)
    part = call(
        functools.partial(attend_kernel, spots, CORES * LAST_BIT),
        jax.ShapeDtypeStruct((half, width + META), BF),
        [VMEM, VMEM, VMEM, VMEM],
    )(kv, q, q_got, lengths.reshape(1, -1))
    got = lax.all_to_all(
        part.reshape(chips, lat_dev, width + META), "ctx", 0, 0, axis_index_groups=same_core
    )
    cols_dev = w_out.shape[1] // heads_axis
    shares = call(
        project_kernel,
        jax.ShapeDtypeStruct((heads_axis, lat_dev, cols_dev), F32),
        [VMEM, VMEM, VMEM],
    )(got, w_out, latents)
    shares = lax.all_to_all(shares, "head", 0, 0, axis_index_groups=[RING])
    return call(finish_kernel, jax.ShapeDtypeStruct((lat_dev, cols_dev), BF), [VMEM])(shares)


def solution(mesh):
    in_specs = (
        P("ctx", None),
        P("ctx", "head"),
        P(),
        P(None, "head"),
        P(None, "head"),
        P(None, "head"),
        P("head", None),
    )
    return jax.shard_map(
        on_device, mesh=mesh, in_specs=in_specs, out_specs=P("ctx", "head"), check_vma=False
    )
```

```python
import functools

import jax
import jax.numpy as jnp
from jax import lax
from jax.experimental import pallas as pl
from jax.experimental.pallas import tpu as pltpu
from jax.sharding import PartitionSpec as P

HD = 128
META = 128
CORES = 2
WV_PARTS = 2
COPY_PARTS = 2
RING = (0, 1, 4, 5, 3, 2, 7, 6)
MASKS = (8, 4, 24, 1, 3)
LAST_BIT = 2
BF = jnp.bfloat16
F32 = jnp.float32
LIMIT = 40 * 1024 * 1024


def split3(a):
    hi = a.astype(BF).astype(F32)
    rest = a - hi
    mid = rest.astype(BF).astype(F32)
    return [hi, mid, (rest - mid).astype(BF).astype(F32)]


def pack_meta(tops, totals):
    rows = tops[0].shape[0]
    lane = lax.broadcasted_iota(jnp.int32, (rows, META), 1)
    meta = jnp.zeros((rows, META), F32)
    column = 0
    for top, total in zip(tops, totals):
        for part in split3(top) + split3(total):
            meta = jnp.where(lane == column, part, meta)
            column += 1
    return meta.astype(BF)


def read_meta(meta, head):
    m = meta.astype(F32)
    part = [m[..., 6 * head + i : 6 * head + i + 1] for i in range(6)]
    return part[0] + (part[1] + part[2]), part[3] + (part[4] + part[5])


def copies_kernel(context, out, held, sems, out_sems):
    parts = sems.shape[0]
    step = held.shape[0] // parts
    rows = [pl.ds(i * step, step) for i in range(parts)]
    fetches = [
        pltpu.make_async_copy(context.at[r], held.at[r], sems.at[i]) for i, r in enumerate(rows)
    ]
    for fetch in fetches:
        fetch.start()
    sends = []
    for i, r in enumerate(rows):
        fetches[i].wait()
        for d in range(out.shape[0]):
            send = pltpu.make_async_copy(held.at[r], out.at[d, r], out_sems.at[i, d])
            send.start()
            sends.append(send)
    for send in sends:
        send.wait()


def key_value_kernel(x, wk, wv_hbm, out, wv, sems):
    width = wk.shape[1]
    step = wv.shape[0] // WV_PARTS
    parts = [pl.ds(i * step, step) for i in range(WV_PARTS)]
    fetches = [
        pltpu.make_async_copy(wv_hbm.at[part], wv.at[part], sems.at[i])
        for i, part in enumerate(parts)
    ]
    for fetch in fetches:
        fetch.start()
    feats = jnp.concatenate([x[RING.index(f)] for f in range(x.shape[0])], axis=1)
    out[:, :width] = jnp.dot(feats, wk[...], preferred_element_type=F32).astype(BF)
    for fetch in fetches:
        fetch.wait()
    out[:, width:] = jnp.dot(feats, wv[...], preferred_element_type=F32).astype(BF)


def attend_kernel(spots, bit, kv, q_own, q_got, lens, out):
    me = lax.axis_index("ctx")
    width = q_own.shape[1]
    positions = kv.shape[0]
    core, base = me % CORES, (me // CORES) * positions
    lower = (me // bit) % 2 == 0
    own, other = q_own[...], q_got[...]
    q = jnp.concatenate([jnp.where(lower, own, other), jnp.where(lower, other, own)], axis=0)
    rows = q.shape[0]
    step = rows // len(spots)
    column = jnp.broadcast_to(lens[...].astype(F32), (8, lens.shape[1])).T[:, :1]
    tiles = [column[i * step : (i + 1) * step] for i in range(CORES * len(spots))]
    last = jnp.concatenate(
        [jnp.where(core == 0, tiles[CORES * p], tiles[CORES * p + 1]) for p in spots], axis=0
    ).astype(jnp.int32)
    visible = base + lax.broadcasted_iota(jnp.int32, (rows, positions), 1) < last
    ones = jnp.ones((positions, HD), BF)
    tops, totals = [], []
    for h in range(width // HD):
        cols = slice(h * HD, (h + 1) * HD)
        s = lax.dot_general(
            q[:, cols], kv[:, cols], (((1,), (1,)), ((), ())), preferred_element_type=F32
        )
        s = jnp.where(visible, s, -jnp.inf)
        top = jnp.maximum(jnp.max(s, axis=1, keepdims=True), -1e30)
        probs = jnp.exp(s - top).astype(BF)
        v = kv[:, width + h * HD : width + (h + 1) * HD]
        both = jnp.dot(probs, jnp.concatenate([v, ones], axis=1), preferred_element_type=F32)
        out[:, cols] = both[:, :HD].astype(BF)
        tops.append(top)
        totals.append(both[:, HD : HD + 1])
    out[:, width:] = pack_meta(tops, totals)


def project_kernel(got, w_out, out):
    width = w_out.shape[0]
    parts = []
    for h in range(width // HD):
        top, total = read_meta(got[:, :, width:], h)
        scale = jnp.exp(top - jnp.max(top, axis=0, keepdims=True))
        o = jnp.sum(scale * got[:, :, h * HD : (h + 1) * HD].astype(F32), axis=0)
        parts.append((o / jnp.sum(scale * total, axis=0)).astype(BF))
    projected = jnp.dot(jnp.concatenate(parts, axis=1), w_out[...], preferred_element_type=F32)
    cols = out.shape[2]
    for at, d in enumerate(RING):
        out[at] = projected[:, d * cols : (d + 1) * cols].astype(BF)


def finish_kernel(shares, latents, out):
    cols = out.shape[1]
    first = pl.multiple_of(lax.axis_index("head") * cols, cols)
    summed = jnp.sum(shares[...].astype(F32), axis=0)
    out[...] = (latents[:, pl.ds(first, cols)].astype(F32) + summed).astype(BF)


VMEM = pl.BlockSpec(memory_space=pltpu.VMEM)
HBM = pl.BlockSpec(memory_space=pltpu.HBM)


def call(kernel, out_shape, in_specs, out_specs=VMEM, scratch=()):
    return pl.pallas_call(
        kernel,
        out_shape=out_shape,
        in_specs=in_specs,
        out_specs=out_specs,
        scratch_shapes=scratch,
        compiler_params=pltpu.CompilerParams(vmem_limit_bytes=LIMIT),
    )


def in_hbm(a):
    return pltpu.with_memory_space_constraint(a, pltpu.HBM)


def on_device(latents, context, lengths, w_query, w_key, w_value, w_out):
    lat_dev = latents.shape[0]
    groups = lax.axis_size("ctx")
    heads_axis = lax.axis_size("head")
    width = w_query.shape[1]
    ctx_dev = context.shape[0]
    chips = groups // CORES
    half = chips * lat_dev
    copies = call(
        copies_kernel,
        jax.ShapeDtypeStruct((heads_axis,) + context.shape, BF),
        [HBM],
        HBM,
        [
            pltpu.VMEM(context.shape, BF),
            pltpu.SemaphoreType.DMA((COPY_PARTS,)),
            pltpu.SemaphoreType.DMA((COPY_PARTS, heads_axis)),
        ],
    )(in_hbm(context))
    x = lax.all_to_all(copies, "head", 0, 0, axis_index_groups=[RING])

    qscale = 1.0 / HD**0.5
    q = (jnp.dot(latents, w_query, preferred_element_type=F32) * qscale).astype(BF)

    masks = [CORES * m for m in MASKS]
    held = [[i] for i in range(groups)]
    for step, mask in enumerate(masks):
        pairs = [
            [i, i ^ mask] for i in range(groups) if min(held[i]) < min(held[i ^ mask])
        ]
        if step < len(masks) - 1:
            q = lax.all_gather(q, "ctx", axis=0, tiled=True, axis_index_groups=pairs)
        for i, j in pairs:
            held[i] = held[j] = held[i] + held[j]
    q_got = lax.ppermute(q, "ctx", [(i, i ^ masks[-1]) for i in range(groups)])
    same_core = [held[c] for c in range(CORES)]
    spots = [d // CORES for d in held[0]]
    core_pairs = [[CORES * g + c for c in range(CORES)] for g in range(chips)]
    kv = call(
        key_value_kernel,
        jax.ShapeDtypeStruct((ctx_dev, 2 * width), BF),
        [VMEM, VMEM, HBM],
        VMEM,
        [pltpu.VMEM(w_value.shape, BF), pltpu.SemaphoreType.DMA((WV_PARTS,))],
    )(x, w_key, in_hbm(w_value))
    kv = lax.all_gather(kv, "ctx", axis=0, tiled=True, axis_index_groups=core_pairs)
    part = call(
        functools.partial(attend_kernel, spots, CORES * LAST_BIT),
        jax.ShapeDtypeStruct((half, width + META), BF),
        [VMEM, VMEM, VMEM, VMEM],
    )(kv, q, q_got, lengths.reshape(1, -1))
    got = lax.all_to_all(
        part.reshape(chips, lat_dev, width + META), "ctx", 0, 0, axis_index_groups=same_core
    )
    cols_dev = w_out.shape[1] // heads_axis
    shares = call(
        project_kernel,
        jax.ShapeDtypeStruct((heads_axis, lat_dev, cols_dev), BF),
        [VMEM, VMEM],
    )(got, w_out)
    shares = lax.all_to_all(shares, "head", 0, 0, axis_index_groups=[RING])
    return call(
        finish_kernel, jax.ShapeDtypeStruct((lat_dev, cols_dev), BF), [VMEM, VMEM]
    )(shares, latents)


def solution(mesh):
    in_specs = (
        P("ctx", None),
        P("ctx", "head"),
        P(),
        P(None, "head"),
        P(None, "head"),
        P(None, "head"),
        P("head", None),
    )
    return jax.shard_map(
        on_device, mesh=mesh, in_specs=in_specs, out_specs=P("ctx", "head"), check_vma=False
    )
```

```python
import functools

import jax
import jax.numpy as jnp
from jax import lax
from jax.experimental import pallas as pl
from jax.experimental.pallas import tpu as pltpu
from jax.sharding import PartitionSpec as P

HD = 128
META = 128
CORES = 2
WV_PARTS = 1
COPY_PARTS = 1
RING = (0, 1, 4, 5, 3, 2, 7, 6)
MASKS = (8, 4, 24, 1, 3)
LAST_BIT = 2
BF = jnp.bfloat16
F32 = jnp.float32
LIMIT = 40 * 1024 * 1024


def split3(a):
    hi = a.astype(BF).astype(F32)
    rest = a - hi
    mid = rest.astype(BF).astype(F32)
    return [hi, mid, (rest - mid).astype(BF).astype(F32)]


def pack_meta(tops, totals):
    rows = tops[0].shape[0]
    lane = lax.broadcasted_iota(jnp.int32, (rows, META), 1)
    meta = jnp.zeros((rows, META), F32)
    column = 0
    for top, total in zip(tops, totals):
        for part in split3(top) + split3(total):
            meta = jnp.where(lane == column, part, meta)
            column += 1
    return meta.astype(BF)


def read_meta(meta, head):
    m = meta.astype(F32)
    part = [m[..., 6 * head + i : 6 * head + i + 1] for i in range(6)]
    return part[0] + (part[1] + part[2]), part[3] + (part[4] + part[5])


def copies_kernel(context, out, held, sems, out_sems):
    parts = sems.shape[0]
    step = held.shape[0] // parts
    rows = [pl.ds(i * step, step) for i in range(parts)]
    fetches = [
        pltpu.make_async_copy(context.at[r], held.at[r], sems.at[i]) for i, r in enumerate(rows)
    ]
    for fetch in fetches:
        fetch.start()
    sends = []
    for i, r in enumerate(rows):
        fetches[i].wait()
        for d in range(out.shape[0]):
            send = pltpu.make_async_copy(held.at[r], out.at[d, r], out_sems.at[i, d])
            send.start()
            sends.append(send)
    for send in sends:
        send.wait()


def key_value_kernel(x, wk, wv_hbm, out, wv, sems):
    width = wk.shape[1]
    step = wv.shape[0] // WV_PARTS
    parts = [pl.ds(i * step, step) for i in range(WV_PARTS)]
    fetches = [
        pltpu.make_async_copy(wv_hbm.at[part], wv.at[part], sems.at[i])
        for i, part in enumerate(parts)
    ]
    for fetch in fetches:
        fetch.start()
    feats = jnp.concatenate([x[RING.index(f)] for f in range(x.shape[0])], axis=1)
    out[:, :width] = jnp.dot(feats, wk[...], preferred_element_type=F32).astype(BF)
    for fetch in fetches:
        fetch.wait()
    out[:, width:] = jnp.dot(feats, wv[...], preferred_element_type=F32).astype(BF)


def attend_kernel(spots, bit, kv, q_own, q_got, lens, out):
    me = lax.axis_index("ctx")
    width = q_own.shape[1]
    positions = kv.shape[0]
    core, base = me % CORES, (me // CORES) * positions
    lower = (me // bit) % 2 == 0
    own, other = q_own[...], q_got[...]
    q = jnp.concatenate([jnp.where(lower, own, other), jnp.where(lower, other, own)], axis=0)
    rows = q.shape[0]
    step = rows // len(spots)
    column = jnp.broadcast_to(lens[...].astype(F32), (8, lens.shape[1])).T[:, :1]
    tiles = [column[i * step : (i + 1) * step] for i in range(CORES * len(spots))]
    last = jnp.concatenate(
        [jnp.where(core == 0, tiles[CORES * p], tiles[CORES * p + 1]) for p in spots], axis=0
    ).astype(jnp.int32)
    visible = base + lax.broadcasted_iota(jnp.int32, (rows, positions), 1) < last
    ones = jnp.ones((positions, HD), BF)
    tops, totals = [], []
    for h in range(width // HD):
        cols = slice(h * HD, (h + 1) * HD)
        s = lax.dot_general(
            q[:, cols], kv[:, cols], (((1,), (1,)), ((), ())), preferred_element_type=F32
        )
        s = jnp.where(visible, s, -jnp.inf)
        top = jnp.maximum(jnp.max(s, axis=1, keepdims=True), -1e30)
        probs = jnp.exp(s - top).astype(BF)
        v = kv[:, width + h * HD : width + (h + 1) * HD]
        both = jnp.dot(probs, jnp.concatenate([v, ones], axis=1), preferred_element_type=F32)
        out[:, cols] = both[:, :HD].astype(BF)
        tops.append(top)
        totals.append(both[:, HD : HD + 1])
    out[:, width:] = pack_meta(tops, totals)


def project_kernel(got, w_out, out):
    width = w_out.shape[0]
    parts = []
    for h in range(width // HD):
        top, total = read_meta(got[:, :, width:], h)
        scale = jnp.exp(top - jnp.max(top, axis=0, keepdims=True))
        o = jnp.sum(scale * got[:, :, h * HD : (h + 1) * HD].astype(F32), axis=0)
        parts.append((o / jnp.sum(scale * total, axis=0)).astype(BF))
    projected = jnp.dot(jnp.concatenate(parts, axis=1), w_out[...], preferred_element_type=F32)
    cols = out.shape[2]
    for at, d in enumerate(RING):
        out[at] = projected[:, d * cols : (d + 1) * cols].astype(BF)


def finish_kernel(shares, latents, out):
    cols = out.shape[1]
    first = pl.multiple_of(lax.axis_index("head") * cols, cols)
    summed = jnp.sum(shares[...].astype(F32), axis=0)
    out[...] = (latents[:, pl.ds(first, cols)].astype(F32) + summed).astype(BF)


VMEM = pl.BlockSpec(memory_space=pltpu.VMEM)
HBM = pl.BlockSpec(memory_space=pltpu.HBM)


def call(kernel, out_shape, in_specs, out_specs=VMEM, scratch=()):
    return pl.pallas_call(
        kernel,
        out_shape=out_shape,
        in_specs=in_specs,
        out_specs=out_specs,
        scratch_shapes=scratch,
        compiler_params=pltpu.CompilerParams(vmem_limit_bytes=LIMIT),
    )


def in_hbm(a):
    return pltpu.with_memory_space_constraint(a, pltpu.HBM)


def on_device(latents, context, lengths, w_query, w_key, w_value, w_out):
    lat_dev = latents.shape[0]
    groups = lax.axis_size("ctx")
    heads_axis = lax.axis_size("head")
    width = w_query.shape[1]
    ctx_dev = context.shape[0]
    chips = groups // CORES
    half = chips * lat_dev
    copies = call(
        copies_kernel,
        jax.ShapeDtypeStruct((heads_axis,) + context.shape, BF),
        [HBM],
        HBM,
        [
            pltpu.VMEM(context.shape, BF),
            pltpu.SemaphoreType.DMA((COPY_PARTS,)),
            pltpu.SemaphoreType.DMA((COPY_PARTS, heads_axis)),
        ],
    )(in_hbm(context))
    x = lax.all_to_all(copies, "head", 0, 0, axis_index_groups=[RING])

    qscale = 1.0 / HD**0.5
    q = (jnp.dot(latents, w_query, preferred_element_type=F32) * qscale).astype(BF)

    masks = [CORES * m for m in MASKS]
    held = [[i] for i in range(groups)]
    for step, mask in enumerate(masks):
        pairs = [
            [i, i ^ mask] for i in range(groups) if min(held[i]) < min(held[i ^ mask])
        ]
        if step < len(masks) - 1:
            q = lax.all_gather(q, "ctx", axis=0, tiled=True, axis_index_groups=pairs)
        for i, j in pairs:
            held[i] = held[j] = held[i] + held[j]
    q_got = lax.ppermute(q, "ctx", [(i, i ^ masks[-1]) for i in range(groups)])
    same_core = [held[c] for c in range(CORES)]
    spots = [d // CORES for d in held[0]]
    core_pairs = [[CORES * g + c for c in range(CORES)] for g in range(chips)]
    kv = call(
        key_value_kernel,
        jax.ShapeDtypeStruct((ctx_dev, 2 * width), BF),
        [VMEM, VMEM, HBM],
        VMEM,
        [pltpu.VMEM(w_value.shape, BF), pltpu.SemaphoreType.DMA((WV_PARTS,))],
    )(x, w_key, in_hbm(w_value))
    kv = lax.all_gather(kv, "ctx", axis=0, tiled=True, axis_index_groups=core_pairs)
    part = call(
        functools.partial(attend_kernel, spots, CORES * LAST_BIT),
        jax.ShapeDtypeStruct((half, width + META), BF),
        [VMEM, VMEM, VMEM, VMEM],
    )(kv, q, q_got, lengths.reshape(1, -1))
    got = lax.all_to_all(
        part.reshape(chips, lat_dev, width + META), "ctx", 0, 0, axis_index_groups=same_core
    )
    cols_dev = w_out.shape[1] // heads_axis
    shares = call(
        project_kernel,
        jax.ShapeDtypeStruct((heads_axis, lat_dev, cols_dev), BF),
        [VMEM, VMEM],
    )(got, w_out)
    shares = lax.all_to_all(shares, "head", 0, 0, axis_index_groups=[RING])
    return call(
        finish_kernel, jax.ShapeDtypeStruct((lat_dev, cols_dev), BF), [VMEM, VMEM]
    )(shares, latents)


def solution(mesh):
    in_specs = (
        P("ctx", None),
        P("ctx", "head"),
        P(),
        P(None, "head"),
        P(None, "head"),
        P(None, "head"),
        P("head", None),
    )
    return jax.shard_map(
        on_device, mesh=mesh, in_specs=in_specs, out_specs=P("ctx", "head"), check_vma=False
    )
```
